32 devices in a mesh: bl: 8 (over z, y), ch: 4 (over x, core).
Axes of the slice: x: 2, y: 2, z: 4, core: 2. Of those that a mesh axis runs over, the one named last changes fastest.
Arguments:
- facet_grid: bfloat16 [4, 64, 16, 1024], P(None, None, None, 'ch'), may hold values from -2 to 2
- kernel: bfloat16 [16384, 1024], P('bl', 'ch'), may hold values from -0.1875 to 0.1875
- tile_of: int32 [32], P('bl'), may hold values from 0 to 3
- observed: bfloat16 [64, 2, 16384], P('ch', None, 'bl'), may hold values from -6 to 6
- flags: int32 [64, 16384], P('ch', 'bl'), may hold values 0 or 1
- pairs: int32 [2, 16384], P(None, 'bl'), may hold values from 0 to 511, as said below
- solver_order: int32 [512], replicated, may hold values from 0 to 511, as said below
Outputs:
- gains: float32 [64, 16, 512], P('ch', None, 'bl')
The draws below stay inside these ranges and needn't reach their ends.
Inputs may be any that keep to these rules, and one draw needn't show every extreme that they name: `solver_order`: each station appears once. `pairs`: for row r, with j = (r mod 2048) // 256, the first station is solver_order[64 * j + m] for some m below 64; the second station differs from the first.
All inputs are finite; a program needn't handle non-finite values. No bound on the sum of `flags` on one device may be relied on, other than what follows from the above.
Results may differ from the reference program's by a relative error of at most 0.013.
Values may be sent and summed in bfloat16 or wider, within the bound.
A program may use at most 128 MiB of HBM per device.

```python
import jax
import jax.numpy as jnp
from jax import lax

S = 512
ND = 8
TILE = 1024
NTILE = 4
BLK = 512
ITERS = 4
VIS_DEV = 2048
NCH = 64
NVIS = 16384
S_DEV = 64
SEG = 256
N_CH = 4


def order_of(key):
    return jax.random.permutation(jax.random.fold_in(key, 11), S).astype(jnp.int32)


def draw_solver_order(key, part):
    return order_of(key)


def draw_pairs(key, part):
    station_order = order_of(key)
    row_index = jnp.arange(NVIS, dtype=jnp.int32)
    segment = row_index % VIS_DEV // SEG
    within = jax.random.randint(jax.random.fold_in(key, 12), (NVIS,), 0, S_DEV, dtype=jnp.int32)
    first_station = station_order[segment * S_DEV + within]
    offset = jax.random.randint(jax.random.fold_in(key, 13), (NVIS,), 1, S, dtype=jnp.int32)
    second_station = (first_station + offset) % S
    return jnp.stack([first_station, second_station]).astype(jnp.int32)


def touch_ends(drawn, own_key, least, largest):
    longest = drawn.shape.index(max(drawn.shape))
    spots = []
    for shift in (0, 1):
        where = [jax.random.randint(jax.random.fold_in(own_key, axis), (), 0, length) for axis, length in enumerate(drawn.shape)]
        where[longest] = (where[longest] + shift) % drawn.shape[longest]
        spots.append(tuple(where))
    return drawn.at[spots[0]].set(least).at[spots[1]].set(largest)


def steps_of(key, shape, shards, smallest, top_value):
    def one(position, shards_of):
        steps = jax.random.uniform(jax.random.fold_in(jax.random.fold_in(key, 6), position), (shards_of,), jnp.float32, smallest / len(shards), top_value / len(shards))
        return jnp.repeat(jnp.exp(steps), shape[position] // shards_of).reshape((-1,) + (1,) * (len(shape) - position - 1))

    level = one(*shards[0])
    for cut in shards[1:]:
        level = level * one(*cut)
    return level


def noise(rng, dims, spread, bound, pieces=(), kind=jnp.bfloat16):
    loudness = steps_of(rng, dims, pieces, -0.22, 0.18) if pieces else 1.0
    values = jax.random.normal(rng, dims, jnp.float32) * spread * loudness
    return jnp.minimum(jnp.maximum(values, -bound), bound).astype(kind)


def setup_inputs(seed: int = 0) -> dict:
    keys = jax.random.split(jax.random.key(seed), 8)
    facet_grid = noise(keys[0], (NTILE, NCH, 2 * ND, TILE), (0.8 * (NVIS // S) ** -0.5), 2.0, ((3, 4),))
    kernel = noise(keys[1], (NVIS, TILE), TILE ** -0.5, 0.1875, ((0, 8), (1, 4)))
    tile_of = touch_ends(jax.random.randint(keys[2], (NVIS // BLK,), 0, NTILE), jax.random.fold_in(keys[2], 1), 0, NTILE - 1).astype(jnp.int32)
    observed = noise(keys[3], (NCH, 2, NVIS), 1.0, 6.0, ((0, 4), (2, 8)))
    flags = touch_ends((jax.random.randint(keys[4], (NCH, NVIS), 0, 8) < 1).astype(jnp.int32), jax.random.fold_in(keys[4], 1), 0, 1)
    pairs = draw_pairs(jax.random.fold_in(keys[7], 71), 0)
    solver_order = draw_solver_order(jax.random.fold_in(keys[7], 71), 0)
    return dict(facet_grid=facet_grid, kernel=kernel, tile_of=tile_of, observed=observed, flags=flags, pairs=pairs, solver_order=solver_order)


def degrid(facet_grid, kernel, tile_of):
    group_width = TILE // N_CH
    kernel_blocks = kernel.reshape(NVIS // BLK, BLK, N_CH, group_width)

    def one_block(inputs):
        tile_index, block_kernel = inputs
        tile_cells = facet_grid[tile_index].astype(jnp.float32).reshape(NCH, 2 * ND, N_CH, group_width)
        group_sums = jnp.einsum('ckgu,vgu->gckv', tile_cells, block_kernel.astype(jnp.float32))
        rounded = lax.optimization_barrier(group_sums.astype(jnp.bfloat16)).astype(jnp.float32)
        return jnp.sum(rounded, axis=0)

    blocks = lax.map(one_block, (tile_of, kernel_blocks))
    return jnp.transpose(blocks, (1, 2, 0, 3)).reshape(NCH, 2 * ND, NVIS)


def channel_sums(inputs, first_slot, second_slot):
    model_row, visible_row, gain_row = inputs
    model_pair = model_row.astype(jnp.float32).reshape(ND, 2, NVIS)
    gain_pair = gain_row.reshape(ND, 2, S)
    model_re = model_pair[:, 0]
    model_im = model_pair[:, 1]
    far_re = gain_pair[:, 0][:, second_slot]
    far_im = gain_pair[:, 1][:, second_slot]
    near_re = gain_pair[:, 0][:, first_slot]
    near_im = gain_pair[:, 1][:, first_slot]
    prod_re = model_re * far_re + model_im * far_im
    prod_im = model_im * far_re - model_re * far_im
    pred_re = jnp.sum(near_re * prod_re - near_im * prod_im, axis=0)
    pred_im = jnp.sum(near_re * prod_im + near_im * prod_re, axis=0)
    vis_pair = visible_row.astype(jnp.float32)
    resid_re = vis_pair[0] - pred_re
    resid_im = vis_pair[1] - pred_im
    empty = jnp.zeros((ND, S), jnp.float32)
    sum_re = empty.at[:, first_slot].add(prod_re * resid_re + prod_im * resid_im)
    sum_im = empty.at[:, first_slot].add(prod_re * resid_im - prod_im * resid_re)
    power = empty.at[:, first_slot].add(prod_re * prod_re + prod_im * prod_im)
    return sum_re, sum_im, power


def reference(facet_grid, kernel, tile_of, observed, flags, pairs, solver_order):
    kept = (1 - flags).astype(jnp.float32)
    model_vis = (degrid(facet_grid, kernel, tile_of) * kept[:, None, :]).astype(jnp.bfloat16)
    visible = (observed.astype(jnp.float32) * kept[:, None, :]).astype(jnp.bfloat16)
    inverse = jnp.zeros((S,), jnp.int32).at[solver_order].set(jnp.arange(S, dtype=jnp.int32))
    first_slot = inverse[pairs[0]].astype(jnp.int32)
    second_slot = inverse[pairs[1]].astype(jnp.int32)
    gains = jnp.zeros((NCH, ND, 2, S), jnp.float32).at[:, :, 0, :].set(1.0).reshape(NCH, 2 * ND, S)
    has_left = (jnp.arange(NCH) > 0).astype(jnp.float32)[:, None, None]
    has_right = (jnp.arange(NCH) < NCH - 1).astype(jnp.float32)[:, None, None]
    for iteration in range(ITERS):
        sum_re, sum_im, power = lax.map(lambda inputs: channel_sums(inputs, first_slot, second_slot), (model_vis, visible, gains))
        gain_pair = gains.reshape(NCH, ND, 2, S)
        gain_re = gain_pair[:, :, 0]
        gain_im = gain_pair[:, :, 1]
        new_re = (sum_re + gain_re * power) / (power + 1.0)
        new_im = (sum_im + gain_im * power) / (power + 1.0)
        averaged = jnp.stack([(gain_re + new_re) * 0.5, (gain_im + new_im) * 0.5], axis=2).reshape(NCH, 2 * ND, S)
        padded = jnp.pad(averaged, ((1, 1), (0, 0), (0, 0)))
        gains = (0.25 * has_left * padded[:-2] + 0.5 * padded[1:-1] + 0.25 * has_right * padded[2:]) / (0.5 + 0.25 * has_left + 0.25 * has_right)
    return gains
```

```python
import functools

import jax
import jax.numpy as jnp
from jax import lax
from jax.experimental import pallas as pl
from jax.experimental.pallas import tpu as pltpu
from jax.sharding import PartitionSpec as P

ND = 8
NK = 2 * ND
ITERS = 4
MESH = pl.DeviceIdType.MESH
F32 = jnp.float32
BF16 = jnp.bfloat16
NN = (((1,), (0,)), ((), ()))
NT = (((1,), (1,)), ((), ()))


def dot(a, b, dims=NN):
    return lax.dot_general(a, b, dims, preferred_element_type=F32)


def one_hot_rows(n):
    row = lax.broadcasted_iota(jnp.int32, (n, n), 0)
    col = lax.broadcasted_iota(jnp.int32, (n, n), 1)
    chan = row // NK
    k = row % NK
    source = chan * NK + (k % ND) * 2 + k // ND
    return (col == source).astype(F32).astype(BF16)


def fused(
    n_bl, n_ch, tile_count,
    tile_of, facet, kern, obs, flags, pairs, order,
    out,
    chosen, send1, recv1, own, recv2, send3, recv3, recvp, far_pick, near_pick,
    gains, h_buf, edge, g_send, g_all, g_lookup,
    s1, r1, s2, r2, s3, r3, sp, rp, sg, rg, se, re,
):
    b = lax.axis_index("bl")
    c = lax.axis_index("ch")
    seg = pairs.shape[2]
    chans = flags.shape[1]
    rows = chans * NK
    owned = out.shape[2]
    blocks = chosen.shape[0]
    segs_per_block = n_bl // blocks if n_bl >= blocks else 1
    par = lax.rem(c, 2)
    hi = lax.div(c, 2)
    mate = c + 1 - 2 * par
    across = (1 - hi) * 2 + par
    right = lax.rem(c + 1, n_ch)
    left = lax.rem(c + n_ch - 1, n_ch)

    def at(i):
        return lax.rem(b + 1 + i, n_bl)

    def back(i):
        return lax.rem(b + 2 * n_bl - 1 - i, n_bl)

    barrier = pltpu.get_barrier_semaphore()
    for step in range(1, n_ch):
        pl.semaphore_signal(
            barrier, inc=1, device_id={"ch": lax.rem(c + step, n_ch)}, device_id_type=MESH
        )

    def greet(i, carry):
        pl.semaphore_signal(barrier, inc=1, device_id={"bl": at(i)}, device_id_type=MESH)
        return carry

    lax.fori_loop(0, n_bl - 1, greet, 0)

    perm = one_hot_rows(rows)
    for block in range(blocks):
        tile = tile_of[block]
        for q in range(n_ch):
            pick = facet[0, q]
            for t in range(1, tile_count):
                pick = jnp.where(tile == t, facet[t, q], pick)
            chosen[block, q] = dot(perm, pick).astype(BF16)

    pl.semaphore_wait(barrier, n_ch - 1 + n_bl - 1)

    def pair_copy(src, dst, sem_s, sem_r, peer):
        return pltpu.make_async_remote_copy(
            src_ref=pairs.at[src], dst_ref=recvp.at[dst], send_sem=sp.at[sem_s],
            recv_sem=rp.at[sem_r], device_id={"bl": peer}, device_id_type=MESH,
        )

    def copy1(j):
        return pltpu.make_async_remote_copy(
            src_ref=send1.at[j], dst_ref=recv1.at[j], send_sem=s1.at[j], recv_sem=r1.at[j],
            device_id={"ch": mate}, device_id_type=MESH,
        )

    def copy2(j):
        return pltpu.make_async_remote_copy(
            src_ref=own.at[j, 1 - hi], dst_ref=recv2.at[j], send_sem=s2.at[j], recv_sem=r2.at[j],
            device_id={"ch": across}, device_id_type=MESH,
        )

    def copy3(src, dst, sem_s, sem_r, peer):
        return pltpu.make_async_remote_copy(
            src_ref=send3.at[src], dst_ref=recv3.at[dst], send_sem=s3.at[sem_s],
            recv_sem=r3.at[sem_r], device_id={"bl": peer}, device_id_type=MESH,
        )

    def gain_copy(it, dst, sem_s, sem_r, peer):
        return pltpu.make_async_remote_copy(
            src_ref=g_send.at[it], dst_ref=g_all.at[it, dst], send_sem=sg.at[it, sem_s],
            recv_sem=rg.at[it, sem_r], device_id={"bl": peer}, device_id_type=MESH,
        )

    def edge_copy(it, side):
        return pltpu.make_async_remote_copy(
            src_ref=h_buf.at[it, (chans - 1) * (1 - side)], dst_ref=edge.at[it, side],
            send_sem=se.at[it, side], recv_sem=re.at[it, side],
            device_id={"ch": right if side == 0 else left}, device_id_type=MESH,
        )

    def send_pairs(i, carry):
        j = at(i)
        pair_copy(j, b, j, b, j).start()
        return carry

    lax.fori_loop(0, n_bl - 1, send_pairs, 0)

    def first(i, carry):
        j = at(i)
        weights = kern[j]
        block = lax.div(j, segs_per_block)
        for half in range(2):
            send1[j, half] = dot(chosen[block, 2 * half + 1 - par], weights, NT).astype(BF16)
        copy1(j).start()
        for half in range(2):
            own[j, half] = dot(chosen[block, 2 * half + par], weights, NT).astype(BF16)
        return carry

    lax.fori_loop(0, n_bl, first, 0)

    def second(i, carry):
        j = at(i)
        copy1(j).wait_recv()
        total = own[j, 1 - hi].astype(F32) + recv1[j, 1 - hi].astype(F32)
        own[j, 1 - hi] = total.astype(BF16)
        copy2(j).start()
        return carry

    lax.fori_loop(0, n_bl, second, 0)

    def picks(s):
        far_pick[s] = (order[...] == recvp[s, 1:2]).astype(F32).astype(BF16)
        mine = order[pl.ds(pl.multiple_of(b * owned, owned), owned)]
        near_pick[s] = (mine == recvp[s, 0:1]).astype(F32).astype(BF16)

    recvp[b] = pairs[b]
    picks(b)

    def take_pairs(i, carry):
        s = back(i)
        pair_copy(b, s, s, s, s).wait_recv()
        picks(s)
        return carry

    lax.fori_loop(0, n_bl - 1, take_pairs, 0)

    def finish(j, target, slot):
        copy2(j).wait_recv()
        kept = (1 - flags[j]).astype(F32)
        total = own[j, hi].astype(F32) + recv1[j, hi].astype(F32) + recv2[j].astype(F32)
        model = total.reshape(chans, NK, seg) * kept[:, None, :]
        target[slot, :rows] = model.reshape(rows, seg).astype(BF16)
        for part in range(2):
            seen = obs[j, part * chans : (part + 1) * chans].astype(F32) * kept
            target[slot, rows + part * chans : rows + (part + 1) * chans] = seen.astype(BF16)

    def third(i, carry):
        j = at(i)
        finish(j, send3, j)
        copy3(j, b, j, b, j).start()
        return carry

    lax.fori_loop(0, n_bl - 1, third, 0)
    finish(b, recv3, b)

    part = lax.broadcasted_iota(jnp.int32, (chans, NK, owned), 1)
    gains[...] = (part < ND).astype(F32)

    chan = lax.broadcasted_iota(jnp.int32, (chans, NK, owned), 0) + c * chans
    has_left = (chan > 0).astype(F32) * 0.25
    has_right = (chan < n_ch * chans - 1).astype(F32) * 0.25

    def terms(it, s, near_hi, near_lo):
        near_one = near_pick[s]
        model = recv3[s, :rows].astype(F32).reshape(chans, NK, seg)
        model_re, model_im = model[:, :ND], model[:, ND:]
        if it == 0:
            prod_re, prod_im = model_re, model_im
            pred_re = jnp.sum(prod_re, axis=1)
            pred_im = jnp.sum(prod_im, axis=1)
        else:
            far = dot(g_lookup[...], far_pick[s]).reshape(chans, NK, seg)
            near = (dot(near_hi, near_one) + dot(near_lo, near_one)).reshape(chans, NK, seg)
            far_re, far_im = far[:, :ND], far[:, ND:]
            near_re, near_im = near[:, :ND], near[:, ND:]
            prod_re = model_re * far_re + model_im * far_im
            prod_im = model_im * far_re - model_re * far_im
            pred_re = jnp.sum(near_re * prod_re - near_im * prod_im, axis=1)
            pred_im = jnp.sum(near_re * prod_im + near_im * prod_re, axis=1)
        res_re = (recv3[s, rows : rows + chans].astype(F32) - pred_re)[:, None, :]
        res_im = (recv3[s, rows + chans : rows + 2 * chans].astype(F32) - pred_im)[:, None, :]
        cross_re = prod_re * res_re + prod_im * res_im
        cross_im = prod_re * res_im - prod_im * res_re
        power = prod_re * prod_re + prod_im * prod_im
        cross = jnp.concatenate([cross_re, cross_im], axis=1).reshape(rows, seg).astype(BF16)
        power = power.reshape(chans * ND, seg).astype(BF16)
        return dot(cross, near_one, NT), dot(power, near_one, NT)

    for it in range(ITERS):
        near_hi = near_lo = None
        if it > 0:
            flat = gains[...].reshape(rows, owned)
            near_hi = flat.astype(BF16)
            near_lo = (flat - near_hi.astype(F32)).astype(BF16)

            def take_gains(i, carry):
                s = back(i)
                gain_copy(it - 1, s, s, s, s).wait_recv()
                return carry

            lax.fori_loop(0, n_bl - 1, take_gains, 0)
            table = g_all[it - 1].astype(F32).reshape(n_bl * owned, rows)
            g_lookup[...] = table.T.astype(BF16)

        def one(i, sums):
            s = back(i)
            if it == 0:

                @pl.when(i < n_bl - 1)
                def _():
                    copy3(s, s, s, s, s).wait_recv()

            more = terms(it, s, near_hi, near_lo)
            return sums[0] + more[0], sums[1] + more[1]

        zeros = (jnp.zeros((rows, owned), F32), jnp.zeros((chans * ND, owned), F32))
        cross, power = lax.fori_loop(0, n_bl, one, zeros)
        gain = gains[...]
        cross = cross.reshape(chans, NK, owned)
        power = power.reshape(chans, ND, owned)
        power = jnp.concatenate([power, power], axis=1)
        h_buf[it] = (gain + (cross + gain * power) / (power + 1.0)) * 0.5
        for side in range(2):
            edge_copy(it, side).start()
        for side in range(2):
            edge_copy(it, side).wait_recv()
        here = h_buf[it]
        before = jnp.concatenate([edge[it, 0:1], here[:-1]], axis=0)
        after = jnp.concatenate([here[1:], edge[it, 1:2]], axis=0)
        gain = (has_left * before + 0.5 * here + has_right * after) / (0.5 + has_left + has_right)
        if it == ITERS - 1:
            out[...] = gain
        else:
            gains[...] = gain
            turned = gain.reshape(rows, owned).T.astype(g_send.dtype)
            g_send[it] = turned

            def spread(i, carry):
                j = at(i)
                gain_copy(it, b, j, b, j).start()
                return carry

            lax.fori_loop(0, n_bl - 1, spread, 0)
            g_all[it, b] = turned

    for it in range(ITERS):
        for side in range(2):
            edge_copy(it, side).wait_send()

    def drain(i, carry):
        j = at(i)
        pair_copy(j, b, j, b, j).wait_send()
        copy3(j, b, j, b, j).wait_send()
        for it in range(ITERS - 1):
            gain_copy(it, b, j, b, j).wait_send()
        return carry

    lax.fori_loop(0, n_bl - 1, drain, 0)

    def drain_sums(j, carry):
        copy1(j).wait_send()
        copy2(j).wait_send()
        return carry

    lax.fori_loop(0, n_bl, drain_sums, 0)


def body(n_bl, n_ch, facet_grid, kernel, tile_of, observed, flags, pairs, solver_order):
    chans = observed.shape[0]
    row_count = observed.shape[2]
    seg = row_count // n_bl
    stations = solver_order.shape[0]
    owned = stations // n_bl
    cells = kernel.shape[1]
    tiles = facet_grid.shape[0]
    blocks = tile_of.shape[0]
    rows = chans * NK
    gdt = BF16 if owned % 16 == 0 else F32
    facet = facet_grid.reshape(tiles, n_ch, rows, cells)
    kern = kernel.reshape(n_bl, seg, cells)
    obs = observed.reshape(chans, 2, n_bl, seg).transpose(2, 1, 0, 3).reshape(n_bl, 2 * chans, seg)
    flag = flags.reshape(chans, n_bl, seg).transpose(1, 0, 2)
    pair = pairs.reshape(2, n_bl, seg).transpose(1, 0, 2)
    vmem = pl.BlockSpec(memory_space=pltpu.VMEM)
    dma = pltpu.SemaphoreType.DMA
    gains = pl.pallas_call(
        functools.partial(fused, n_bl, n_ch, tiles),
        out_shape=jax.ShapeDtypeStruct((chans, NK, owned), F32),
        in_specs=[pl.BlockSpec(memory_space=pltpu.SMEM)] + [vmem] * 6,
        out_specs=vmem,
        scratch_shapes=[
            pltpu.VMEM((blocks, n_ch, rows, cells), BF16),
            pltpu.VMEM((n_bl, 2, rows, seg), BF16),
            pltpu.VMEM((n_bl, 2, rows, seg), BF16),
            pltpu.VMEM((n_bl, 2, rows, seg), BF16),
            pltpu.VMEM((n_bl, rows, seg), BF16),
            pltpu.VMEM((n_bl, rows + 2 * chans, seg), BF16),
            pltpu.VMEM((n_bl, rows + 2 * chans, seg), BF16),
            pltpu.VMEM((n_bl, 2, seg), jnp.int32),
            pltpu.VMEM((n_bl, stations, seg), BF16),
            pltpu.VMEM((n_bl, owned, seg), BF16),
            pltpu.VMEM((chans, NK, owned), F32),
            pltpu.VMEM((ITERS, chans, NK, owned), F32),
            pltpu.VMEM((ITERS, 2, NK, owned), F32),
            pltpu.VMEM((ITERS - 1, owned, rows), gdt),
            pltpu.VMEM((ITERS - 1, n_bl, owned, rows), gdt),
            pltpu.VMEM((rows, stations), BF16),
        ]
        + [dma((n_bl,))] * 8
        + [dma((ITERS - 1, n_bl))] * 2
        + [dma((ITERS, 2))] * 2,
        compiler_params=pltpu.CompilerParams(
            collective_id=0, has_side_effects=True, vmem_limit_bytes=60 * 1024 * 1024
        ),
        name="calibrate",
    )(tile_of, facet, kern, obs, flag, pair, solver_order.reshape(stations, 1))
    return gains.reshape(chans, 2, ND, owned).transpose(0, 2, 1, 3).reshape(chans, NK, owned)


def solution(mesh):
    in_specs = (
        P(None, None, None, "ch"),
        P("bl", "ch"),
        P("bl"),
        P("ch", None, "bl"),
        P("ch", "bl"),
        P(None, "bl"),
        P(),
    )
    out_specs = P("ch", None, "bl")
    local = functools.partial(body, mesh.shape["bl"], mesh.shape["ch"])
    return jax.shard_map(local, mesh=mesh, in_specs=in_specs, out_specs=out_specs, check_vma=False)
```

```python
import functools

import jax
import jax.numpy as jnp
from jax import lax
from jax.experimental import pallas as pl
from jax.experimental.pallas import tpu as pltpu
from jax.sharding import PartitionSpec as P

ND = 8
NK = 2 * ND
ITERS = 4
MESH = pl.DeviceIdType.MESH
F32 = jnp.float32
BF16 = jnp.bfloat16
NN = (((1,), (0,)), ((), ()))
NT = (((1,), (1,)), ((), ()))


def dot(a, b, dims=NN):
    return lax.dot_general(a, b, dims, preferred_element_type=F32)


def one_hot_rows(n):
    row = lax.broadcasted_iota(jnp.int32, (n, n), 0)
    col = lax.broadcasted_iota(jnp.int32, (n, n), 1)
    chan = row // NK
    k = row % NK
    source = chan * NK + (k % ND) * 2 + k // ND
    return (col == source).astype(F32).astype(BF16)


def fused(
    n_bl, n_ch, tile_count,
    tile_of, facet, kern, obs, flags, pairs, order_row,
    out,
    chosen, send1, recv1, own, recv2, send3, recv3, recvp, far_pick, near_pick,
    gains, h_buf, edge, g_all, g_lookup, order,
    s1, r1, s2, r2, s3, r3, sp, rp, sg, rg, se, re,
):
    b = lax.axis_index("bl")
    c = lax.axis_index("ch")
    seg = pairs.shape[2]
    chans = flags.shape[1]
    rows = chans * NK
    owned = out.shape[2]
    blocks = chosen.shape[0]
    segs_per_block = n_bl // blocks if n_bl >= blocks else 1
    par = lax.rem(c, 2)
    hi = lax.div(c, 2)
    mate = c + 1 - 2 * par
    across = (1 - hi) * 2 + par
    right = lax.rem(c + 1, n_ch)
    left = lax.rem(c + n_ch - 1, n_ch)

    def at(i):
        return lax.rem(b + 1 + i, n_bl)

    def back(i):
        return lax.rem(b + 2 * n_bl - 1 - i, n_bl)

    barrier = pltpu.get_barrier_semaphore()
    for step in range(1, n_ch):
        pl.semaphore_signal(
            barrier, inc=1, device_id={"ch": lax.rem(c + step, n_ch)}, device_id_type=MESH
        )

    def greet(i, carry):
        pl.semaphore_signal(barrier, inc=1, device_id={"bl": at(i)}, device_id_type=MESH)
        return carry

    lax.fori_loop(0, n_bl - 1, greet, 0)

    width = min(128, order_row.shape[1])
    diagonal = lax.broadcasted_iota(jnp.int32, (width, width), 0) == lax.broadcasted_iota(
        jnp.int32, (width, width), 1
    )
    for start in range(0, order_row.shape[1], width):
        line = order_row[:, start : start + width].astype(F32)
        column = jnp.sum(jnp.where(diagonal, line, 0.0), axis=1, keepdims=True)
        order[start : start + width] = column.astype(jnp.int32)

    perm = one_hot_rows(rows)
    for block in range(blocks):
        tile = tile_of[block]
        for q in range(n_ch):
            pick = facet[0, q]
            for t in range(1, tile_count):
                pick = jnp.where(tile == t, facet[t, q], pick)
            chosen[block, q] = dot(perm, pick).astype(BF16)

    pl.semaphore_wait(barrier, n_ch - 1 + n_bl - 1)

    def pair_copy(src, dst, sem_s, sem_r, peer):
        return pltpu.make_async_remote_copy(
            src_ref=pairs.at[src], dst_ref=recvp.at[dst], send_sem=sp.at[sem_s],
            recv_sem=rp.at[sem_r], device_id={"bl": peer}, device_id_type=MESH,
        )

    def copy1(j):
        return pltpu.make_async_remote_copy(
            src_ref=send1.at[j], dst_ref=recv1.at[j], send_sem=s1.at[j], recv_sem=r1.at[j],
            device_id={"ch": mate}, device_id_type=MESH,
        )

    def copy2(j):
        return pltpu.make_async_remote_copy(
            src_ref=own.at[j, 1 - hi], dst_ref=recv2.at[j], send_sem=s2.at[j], recv_sem=r2.at[j],
            device_id={"ch": across}, device_id_type=MESH,
        )

    def copy3(src, dst, sem_s, sem_r, peer):
        return pltpu.make_async_remote_copy(
            src_ref=send3.at[src], dst_ref=recv3.at[dst], send_sem=s3.at[sem_s],
            recv_sem=r3.at[sem_r], device_id={"bl": peer}, device_id_type=MESH,
        )

    def gain_copy(it, held, sem_s, peer):
        return pltpu.make_async_remote_copy(
            src_ref=g_all.at[it, held], dst_ref=g_all.at[it, held], send_sem=sg.at[it, sem_s],
            recv_sem=rg.at[it, held], device_id={"bl": peer}, device_id_type=MESH,
        )

    def edge_copy(it, side):
        return pltpu.make_async_remote_copy(
            src_ref=h_buf.at[it, (chans - 1) * (1 - side)], dst_ref=edge.at[it, side],
            send_sem=se.at[it, side], recv_sem=re.at[it, side],
            device_id={"ch": right if side == 0 else left}, device_id_type=MESH,
        )

    def send_pairs(i, carry):
        j = at(i)
        pair_copy(j, b, j, b, j).start()
        return carry

    lax.fori_loop(0, n_bl - 1, send_pairs, 0)

    def first(i, carry):
        j = at(i)
        weights = kern[j]
        block = lax.div(j, segs_per_block)
        for half in range(2):
            send1[j, half] = dot(chosen[block, 2 * half + 1 - par], weights, NT).astype(BF16)
        copy1(j).start()
        for half in range(2):
            own[j, half] = dot(chosen[block, 2 * half + par], weights, NT).astype(BF16)
        return carry

    lax.fori_loop(0, n_bl, first, 0)

    def second(i, carry):
        j = at(i)
        copy1(j).wait_recv()
        total = own[j, 1 - hi].astype(F32) + recv1[j, 1 - hi].astype(F32)
        own[j, 1 - hi] = total.astype(BF16)
        copy2(j).start()
        return carry

    lax.fori_loop(0, n_bl, second, 0)

    def picks(s):
        far_pick[s] = (order[...] == recvp[s, 1:2]).astype(F32).astype(BF16)
        mine = order[pl.ds(pl.multiple_of(b * owned, owned), owned)]
        mine = jnp.concatenate([mine, mine], axis=0)
        near_pick[s] = (mine == recvp[s, 0:1]).astype(F32).astype(BF16)

    recvp[b] = pairs[b]
    picks(b)

    def take_pairs(i, carry):
        s = back(i)
        pair_copy(b, s, s, s, s).wait_recv()
        picks(s)
        return carry

    lax.fori_loop(0, n_bl - 1, take_pairs, 0)

    def finish(j, target, slot):
        copy2(j).wait_recv()
        kept = (1 - flags[j]).astype(F32)
        total = own[j, hi].astype(F32) + recv1[j, hi].astype(F32) + recv2[j].astype(F32)
        model = total.reshape(chans, NK, seg) * kept[:, None, :]
        target[slot, :rows] = model.reshape(rows, seg).astype(BF16)
        for part in range(2):
            seen = obs[j, part * chans : (part + 1) * chans].astype(F32) * kept
            target[slot, rows + part * chans : rows + (part + 1) * chans] = seen.astype(BF16)

    def third(i, carry):
        j = at(i)
        finish(j, send3, j)
        copy3(j, b, j, b, j).start()
        return carry

    lax.fori_loop(0, n_bl - 1, third, 0)
    finish(b, recv3, b)

    part = lax.broadcasted_iota(jnp.int32, (chans, NK, owned), 1)
    gains[...] = (part < ND).astype(F32)

    chan = lax.broadcasted_iota(jnp.int32, (chans, NK, owned), 0) + c * chans
    has_left = (chan > 0).astype(F32) * 0.25
    has_right = (chan < n_ch * chans - 1).astype(F32) * 0.25

    def terms(it, s, near_gain):
        near_two = near_pick[s]
        near_one = near_two[:owned]
        model = recv3[s, :rows].astype(F32).reshape(chans, NK, seg)
        model_re, model_im = model[:, :ND], model[:, ND:]
        if it == 0:
            prod_re, prod_im = model_re, model_im
            pred_re = jnp.sum(prod_re, axis=1)
            pred_im = jnp.sum(prod_im, axis=1)
        else:
            far = dot(g_lookup[...], far_pick[s]).reshape(chans, NK, seg)
            near = dot(near_gain, near_two).reshape(chans, NK, seg)
            far_re, far_im = far[:, :ND], far[:, ND:]
            near_re, near_im = near[:, :ND], near[:, ND:]
            prod_re = model_re * far_re + model_im * far_im
            prod_im = model_im * far_re - model_re * far_im
            pred_re = jnp.sum(near_re * prod_re - near_im * prod_im, axis=1)
            pred_im = jnp.sum(near_re * prod_im + near_im * prod_re, axis=1)
        res_re = (recv3[s, rows : rows + chans].astype(F32) - pred_re)[:, None, :]
        res_im = (recv3[s, rows + chans : rows + 2 * chans].astype(F32) - pred_im)[:, None, :]
        cross_re = prod_re * res_re + prod_im * res_im
        cross_im = prod_re * res_im - prod_im * res_re
        power = prod_re * prod_re + prod_im * prod_im
        cross = jnp.concatenate([cross_re, cross_im], axis=1).reshape(rows, seg).astype(BF16)
        power = power.reshape(chans * ND, seg).astype(BF16)
        return dot(cross, near_one, NT), dot(power, near_one, NT)

    for it in range(ITERS):
        near_gain = None
        if it > 0:
            flat = gains[...].reshape(rows, owned)
            near_hi = flat.astype(BF16)
            near_lo = (flat - near_hi.astype(F32)).astype(BF16)
            near_gain = jnp.concatenate([near_hi, near_lo], axis=1)

            def take_gains(i, carry):
                s = back(i)
                gain_copy(it - 1, s, s, s).wait_recv()
                return carry

            lax.fori_loop(0, n_bl - 1, take_gains, 0)
            table = g_all[it - 1].astype(F32).reshape(n_bl * owned, rows)
            g_lookup[...] = table.T.astype(BF16)

        def one(i, sums):
            s = back(i)
            if it == 0:

                @pl.when(i < n_bl - 1)
                def _():
                    copy3(s, s, s, s, s).wait_recv()

            more = terms(it, s, near_gain)
            return sums[0] + more[0], sums[1] + more[1]

        zeros = (jnp.zeros((rows, owned), F32), jnp.zeros((chans * ND, owned), F32))
        cross, power = lax.fori_loop(0, n_bl, one, zeros)
        gain = gains[...]
        cross = cross.reshape(chans, NK, owned)
        power = power.reshape(chans, ND, owned)
        power = jnp.concatenate([power, power], axis=1)
        h_buf[it] = (gain + (cross + gain * power) / (power + 1.0)) * 0.5
        for side in range(2):
            edge_copy(it, side).start()
        for side in range(2):
            edge_copy(it, side).wait_recv()
        here = h_buf[it]
        before = jnp.concatenate([edge[it, 0:1], here[:-1]], axis=0)
        after = jnp.concatenate([here[1:], edge[it, 1:2]], axis=0)
        gain = (has_left * before + 0.5 * here + has_right * after) / (0.5 + has_left + has_right)
        if it == ITERS - 1:
            out[...] = gain
        else:
            gains[...] = gain
            g_all[it, b] = gain.reshape(rows, owned).T.astype(g_all.dtype)

            def spread(i, carry):
                j = at(i)
                gain_copy(it, b, j, j).start()
                return carry

            lax.fori_loop(0, n_bl - 1, spread, 0)

    for it in range(ITERS):
        for side in range(2):
            edge_copy(it, side).wait_send()

    def drain(i, carry):
        j = at(i)
        pair_copy(j, b, j, b, j).wait_send()
        copy3(j, b, j, b, j).wait_send()
        for it in range(ITERS - 1):
            gain_copy(it, b, j, j).wait_send()
        return carry

    lax.fori_loop(0, n_bl - 1, drain, 0)

    def drain_sums(j, carry):
        copy1(j).wait_send()
        copy2(j).wait_send()
        return carry

    lax.fori_loop(0, n_bl, drain_sums, 0)


def body(n_bl, n_ch, facet_grid, kernel, tile_of, observed, flags, pairs, solver_order):
    chans = observed.shape[0]
    row_count = observed.shape[2]
    seg = row_count // n_bl
    stations = solver_order.shape[0]
    owned = stations // n_bl
    cells = kernel.shape[1]
    tiles = facet_grid.shape[0]
    blocks = tile_of.shape[0]
    rows = chans * NK
    gdt = BF16 if owned % 16 == 0 else F32
    facet = facet_grid.reshape(tiles, n_ch, rows, cells)
    kern = kernel.reshape(n_bl, seg, cells)
    obs = observed.reshape(chans, 2, n_bl, seg).transpose(2, 1, 0, 3).reshape(n_bl, 2 * chans, seg)
    flag = flags.reshape(chans, n_bl, seg).transpose(1, 0, 2)
    pair = pairs.reshape(2, n_bl, seg).transpose(1, 0, 2)
    vmem = pl.BlockSpec(memory_space=pltpu.VMEM)
    dma = pltpu.SemaphoreType.DMA
    gains = pl.pallas_call(
        functools.partial(fused, n_bl, n_ch, tiles),
        out_shape=jax.ShapeDtypeStruct((chans, NK, owned), F32),
        in_specs=[pl.BlockSpec(memory_space=pltpu.SMEM)] + [vmem] * 6,
        out_specs=vmem,
        scratch_shapes=[
            pltpu.VMEM((blocks, n_ch, rows, cells), BF16),
            pltpu.VMEM((n_bl, 2, rows, seg), BF16),
            pltpu.VMEM((n_bl, 2, rows, seg), BF16),
            pltpu.VMEM((n_bl, 2, rows, seg), BF16),
            pltpu.VMEM((n_bl, rows, seg), BF16),
            pltpu.VMEM((n_bl, rows + 2 * chans, seg), BF16),
            pltpu.VMEM((n_bl, rows + 2 * chans, seg), BF16),
            pltpu.VMEM((n_bl, 2, seg), jnp.int32),
            pltpu.VMEM((n_bl, stations, seg), BF16),
            pltpu.VMEM((n_bl, 2 * owned, seg), BF16),
            pltpu.VMEM((chans, NK, owned), F32),
            pltpu.VMEM((ITERS, chans, NK, owned), F32),
            pltpu.VMEM((ITERS, 2, NK, owned), F32),
            pltpu.VMEM((ITERS - 1, n_bl, owned, rows), gdt),
            pltpu.VMEM((rows, stations), BF16),
            pltpu.VMEM((stations, 1), jnp.int32),
        ]
        + [dma((n_bl,))] * 8
        + [dma((ITERS - 1, n_bl))] * 2
        + [dma((ITERS, 2))] * 2,
        compiler_params=pltpu.CompilerParams(
            collective_id=0, has_side_effects=True, vmem_limit_bytes=60 * 1024 * 1024
        ),
        name="calibrate",
    )(tile_of, facet, kern, obs, flag, pair, solver_order.reshape(1, stations))
    return gains.reshape(chans, 2, ND, owned).transpose(0, 2, 1, 3).reshape(chans, NK, owned)


def solution(mesh):
    in_specs = (
        P(None, None, None, "ch"),
        P("bl", "ch"),
        P("bl"),
        P("ch", None, "bl"),
        P("ch", "bl"),
        P(None, "bl"),
        P(),
    )
    out_specs = P("ch", None, "bl")
    local = functools.partial(body, mesh.shape["bl"], mesh.shape["ch"])
    return jax.shard_map(local, mesh=mesh, in_specs=in_specs, out_specs=out_specs, check_vma=False)
```
